256 devices in a mesh: pipe: 8 (over y, x_lo), expert: 32 (over z, x_hi, core).
Axes of the slice: x: 4 (x_hi: 2, x_lo: 2; x = x_hi * 2 + x_lo), y: 4, z: 8, core: 2. Of those that a mesh axis runs over, the one named last changes fastest.
Arguments:
- fwd_tokens: bfloat16 [8, 2048, 3584], P('pipe', 'expert'), may hold values from -6 to 6
- bwd_tokens: bfloat16 [8, 2048, 3584], P('pipe', 'expert'), may hold values from -6 to 6
- routes: int32 [8, 32, 128, 2], P('pipe', 'expert'), may hold values from 0 to 15, all different within a row; in each aligned block of 128 rows (0 to 127, 128 to 255, ..., all dimensions but the last counted through in order) at most 20 rows name the same one
- route_weights: float32 [8, 32, 128, 2], P('pipe', 'expert'), may hold values from 0.2 to 1
- norm_gain: float32 [8, 3584], P('pipe'), may hold values from 0.5 to 1.5
- gate_up: bfloat16 [8, 32, 3584, 1024], P('pipe', 'expert'), may hold values from -0.09375 to 0.09375
- down: bfloat16 [8, 32, 512, 3584], P('pipe', 'expert'), may hold values from -0.1875 to 0.1875
Outputs:
- fwd_next: bfloat16 [8, 2048, 3584], P('pipe', 'expert')
- bwd_next: bfloat16 [8, 2048, 3584], P('pipe', 'expert')
The draws below stay inside these ranges and needn't reach their ends.
Inputs may be any that keep to these rules, and one draw needn't show every extreme that they name: In each block [s, e] of 128 rows at most 20 routes name one expert, and some block reaches 20; a token's 2 routes name different experts.
All inputs are finite; a program needn't handle non-finite values.
Results may differ from the reference program's by a relative error of at most 0.0049.
Values may be sent and summed in bfloat16 or wider, within the bound.
No kernel may reach another device: no remote copies, remote signals or barrier semaphores. Data moves between devices by JAX's collectives and lax.ppermute only.
A program may use at most 64 MiB of HBM per device.

```python
import math
import jax
import jax.numpy as jnp
import numpy as np
from jax import lax

D = 3584
H = 1024
TOK_DEV = 128
TOPW = 2
SECTIONS = 8
HALF = 64
MB_TOK = 2048
CAP = 20
N_EXPERT = 32


def shard_levels(own_key, shape, pieces, low, top_value):
    level, own = 1.0, jax.random.fold_in(own_key, 6)
    for axis_at, parts in pieces:
        steps = jnp.exp(jax.random.uniform(jax.random.fold_in(own, axis_at), (parts,), jnp.float32, low / len(pieces), top_value / len(pieces)))
        level = level * jnp.repeat(steps, shape[axis_at] // parts).reshape([-1 if axis == axis_at else 1 for axis in range(len(shape))])
    return level


def shared_out(rng, own, number, rows, number_of, top, limit, skew):
    order = jax.random.permutation(rng, number_of)
    heavy_load, usual = load_shares(number_of, rows * top, limit, skew, True), load_shares(number_of, rows * top, limit, skew, False)
    places = jnp.arange(number_of)

    def named(tallies, turn):
        used = int((tallies > 0).sum())
        fixed = max(1, used // 4)
        shifted = fixed + (places - fixed + turn * (used - fixed)) % max(1, number_of - fixed)
        return jnp.zeros((number_of,), jnp.int32).at[order[jnp.where(places < fixed, places, shifted)]].set(jnp.asarray(tallies, jnp.int32))

    tallies = jnp.where(number % 4 == 0, named(heavy_load, number // 4), named(usual, number - number // 4 - 1))
    mixed = jax.random.permutation(jax.random.fold_in(own, 3), number_of)
    giver, receiver = mixed[0:number_of // 2 * 2:2], mixed[1:number_of // 2 * 2:2]
    margin = jnp.minimum(tallies[giver] - 1, limit - tallies[receiver]) // 2
    margin = jnp.where((giver == order[0]) | (receiver == order[0]) | (tallies[receiver] == 0), 0, jnp.maximum(margin, 0))
    shifted = jax.random.randint(jax.random.fold_in(own, 4), (number_of // 2,), 0, 1 << 20) % (margin + 1)
    tallies = tallies.at[giver].add(-shifted).at[receiver].add(shifted)
    items = jnp.searchsorted(jnp.cumsum(tallies), jnp.arange(rows * top), side="right").astype(jnp.int32)
    table = items.reshape(top, rows).T
    table = table[jax.random.permutation(jax.random.fold_in(own, 1), rows)]
    turn = jax.random.randint(jax.random.fold_in(own, 2), (rows, 1), 0, top)
    return jnp.take_along_axis(table, (jnp.arange(top)[None, :] + turn) % top, axis=1)


def load_shares(amount, total, most, slope, full):
    portions = [(1 << 20) // math.isqrt(standing ** slope) + 1 for standing in range(1, amount + 1)]
    largest = most if full else min(most, max(-(-total // amount), total * portions[0] // sum(portions)))
    least = 1 if total - largest >= amount - 1 else 0
    given, rest = [largest] + [least] * (amount - 1), total - largest - least * (amount - 1)
    while rest > 0:
        movable = [i for i in range(1, amount) if given[i] < largest] or [i for i in range(1, amount) if given[i] < most]
        whole, budget = sum([portions[i] for i in movable]), rest
        for i in movable:
            more = min(most - given[i], max(1, budget * portions[i] // whole), rest)
            given[i] = given[i] + more
            rest = rest - more
    return np.array(given)


def normal_values(rng, shape, scale, bound, shards=(), held_as=jnp.bfloat16):
    values = jax.random.normal(rng, shape, jnp.float32) * scale
    if len(shards) > 0:
        values = shard_levels(rng, shape, shards, -0.22, 0.18) * values
    return jnp.clip(values, min=-bound, max=bound).astype(held_as)


def setup_inputs(seed: int = 0) -> dict:
    key_list = jax.random.split(jax.random.key(seed), 8)
    fwd_tokens = normal_values(key_list[0], (SECTIONS, MB_TOK, D), 1.0, 6.0, ((0, 8), (1, 32)))
    bwd_tokens = normal_values(key_list[1], (SECTIONS, MB_TOK, D), 1.0, 6.0, ((0, 8), (1, 32)))
    routes_keys = jax.random.split(jax.random.fold_in(key_list[2], 1), SECTIONS * N_EXPERT * TOK_DEV // TOK_DEV)
    routes_turns = jax.random.permutation(jax.random.fold_in(key_list[2], 3), SECTIONS * N_EXPERT * TOK_DEV // TOK_DEV)
    routes = jax.vmap(lambda own, number: shared_out(jax.random.fold_in(key_list[2], 2), own, number, TOK_DEV, N_EXPERT // 2, TOPW, CAP, 2))(routes_keys, routes_turns).reshape((SECTIONS, N_EXPERT, TOK_DEV, TOPW))
    route_weights = jnp.clip(0.2 + 0.8 * jax.random.uniform(key_list[3], (SECTIONS, N_EXPERT, TOK_DEV, TOPW), jnp.float32) ** shard_levels(key_list[3], (SECTIONS, N_EXPERT, TOK_DEV, TOPW), ((0, 8), (1, 32)), -0.2, 0.2), 0.2, 1.0)
    norm_gain = jnp.clip(1.0 + 0.1 * jax.random.normal(key_list[4], (SECTIONS, D), jnp.float32), 0.5, 1.5)
    gate_up = normal_values(key_list[5], (SECTIONS, N_EXPERT, D, H), D ** -0.5, 0.09375, ((0, 8), (1, 32)))
    down = normal_values(key_list[6], (SECTIONS, N_EXPERT, H // 2, D), H ** -0.5, 0.1875, ((0, 8), (1, 32)))
    return {"fwd_tokens": fwd_tokens, "bwd_tokens": bwd_tokens, "routes": routes, "route_weights": route_weights, "norm_gain": norm_gain, "gate_up": gate_up, "down": down}


def rms_rows(rows, gain):
    values = rows.astype(jnp.float32)
    scale = lax.rsqrt(lax.optimization_barrier(jnp.mean(values * values, axis=-1, keepdims=True)) + 1e-06)
    return (values * scale * gain).astype(jnp.bfloat16)

def slot_ranks(route_ids, experts):
    flat_ids = route_ids.reshape(-1)
    onehot = (flat_ids[:, None] == jnp.arange(experts, dtype=jnp.int32)[None, :]).astype(jnp.int32)
    earlier = jnp.cumsum(onehot, axis=0) - onehot
    return lax.optimization_barrier(jnp.sum(earlier * onehot, axis=1)).astype(jnp.int32)

def slot_owners(route_ids, experts, capacity):
    flat_ids = route_ids.reshape(-1)
    ranks = slot_ranks(route_ids, experts)
    top = route_ids.shape[-1]
    owners = jnp.arange(flat_ids.shape[0], dtype=jnp.int32) // top + 1
    match = (flat_ids[:, None, None] == jnp.arange(experts, dtype=jnp.int32)[None, :, None]) & (ranks[:, None, None] == jnp.arange(capacity, dtype=jnp.int32)[None, None, :])
    return (lax.optimization_barrier(jnp.sum(match.astype(jnp.int32) * owners[:, None, None], axis=0)) - 1).astype(jnp.int32)

def half_expert(picked, weights_up, weights_down):
    hidden_half = weights_down.shape[0]
    pre = jnp.dot(picked, weights_up, preferred_element_type=jnp.float32)
    hidden = (jax.nn.silu(pre[:, :hidden_half]) * pre[:, hidden_half:]).astype(jnp.bfloat16)
    return jnp.dot(hidden, weights_down, preferred_element_type=jnp.float32).astype(jnp.bfloat16)

def reference(fwd_tokens, bwd_tokens, routes, route_weights, norm_gain, gate_up, down):
    groups = N_EXPERT
    experts = groups // 2
    out_fwd = []
    out_bwd = []
    for section in range(SECTIONS):
        rows = jnp.concatenate([fwd_tokens[section].reshape(groups, HALF, D), bwd_tokens[section].reshape(groups, HALF, D)], axis=1)
        normed = rms_rows(rows, norm_gain[section])
        owners = jax.vmap(lambda ids: slot_owners(ids, experts, CAP))(routes[section])
        ranks = jax.vmap(lambda ids: slot_ranks(ids, experts))(routes[section]).reshape(groups, TOK_DEV, TOPW)
        pair_up = gate_up[section].reshape(experts, 2, D, H)
        pair_down = down[section].reshape(experts, 2, H // 2, D)
        owner_by_expert = jnp.transpose(owners, (1, 0, 2))

        def run_expert(operands):
            weights_up, weights_down, owner = operands
            valid = owner >= 0
            picked = normed[jnp.arange(groups)[:, None], jnp.maximum(owner, 0)]
            picked = jnp.where(valid[..., None], picked, jnp.zeros_like(picked)).reshape(groups * CAP, D)
            out_low = half_expert(picked, weights_up[0], weights_down[0])
            out_high = half_expert(picked, weights_up[1], weights_down[1])
            total = out_low.astype(jnp.float32) + out_high.astype(jnp.float32)
            return total.reshape(groups, CAP, D)
        outputs = lax.map(run_expert, (pair_up, pair_down, owner_by_expert))
        chosen = outputs[routes[section], jnp.arange(groups)[:, None, None], ranks]
        mixed = lax.optimization_barrier(jnp.sum(route_weights[section][..., None] * chosen, axis=2))
        updated = (rows.astype(jnp.float32) + mixed).astype(jnp.bfloat16)
        out_fwd.append(updated[:, :HALF].reshape(groups * HALF, D))
        out_bwd.append(updated[:, HALF:].reshape(groups * HALF, D))
    fwd_all = jnp.stack(out_fwd, axis=0)
    bwd_all = jnp.stack(out_bwd, axis=0)
    return (jnp.roll(fwd_all, 1, axis=0), jnp.roll(bwd_all, -1, axis=0))
```

```python
import functools
import jax
import jax.numpy as jnp
from jax import lax
from jax.experimental import pallas as pl
from jax.experimental.pallas import tpu as pltpu
from jax.sharding import PartitionSpec as P

D = 3584
H2 = 512
TOK = 128
HALF = 64
CHIPS = 16
MAIN = 16
REST = 4
QUART = D // 4
WIDE = D + QUART
META = 16
GROUPS = ((0, 1, 2, 3, 4, 5, 6, 7), (8, 9, 10, 11, 12, 13, 14, 15))
ORDER = ((0, 0), (0, 1), (1, 0), (7, 0), (1, 1), (7, 1), (2, 0), (6, 0), (2, 1), (6, 1), (3, 0), (5, 0), (3, 1), (5, 1), (4, 0), (4, 1))
VMEM = pl.BlockSpec(memory_space=pltpu.VMEM)
SMEM = pl.BlockSpec(memory_space=pltpu.SMEM)
F32 = jnp.float32
BF16 = jnp.bfloat16


def iota(shape, axis):
    return lax.broadcasted_iota(jnp.int32, shape, axis)


def call(kernel, out_shape, in_specs, out_specs, scratch=(), limit=56):
    return pl.pallas_call(
        kernel,
        out_shape=out_shape,
        in_specs=in_specs,
        out_specs=out_specs,
        scratch_shapes=scratch,
        compiler_params=pltpu.CompilerParams(vmem_limit_bytes=limit * 2**20),
    )


def build_kernel(place, fwd, bwd, ids, weights, gain, *outs):
    blocks, carried = outs[:CHIPS], outs[CHIPS]
    z, xh = place[0], place[1]
    carried[0:HALF, :] = fwd[...]
    carried[HALF:TOK, :] = bwd[...]
    rows = carried[0:TOK, :].astype(F32)
    scale = lax.rsqrt(jnp.mean(rows * rows, axis=-1, keepdims=True) + 1e-06)
    normed = (rows * scale * gain[...]).astype(BF16)
    id_cols = ids[...].astype(F32)
    w_cols = weights[...]
    high = w_cols.astype(BF16).astype(F32)
    low = (w_cols - high).astype(BF16).astype(F32)
    lane = iota((TOK, 128), 1)
    table = jnp.zeros((TOK, 128), F32)
    for at, column in enumerate((id_cols[:, 0:1], id_cols[:, 1:2], high[:, 0:1], high[:, 1:2], low[:, 0:1], low[:, 1:2])):
        table = jnp.where(lane == at, column, table)
    eye = (iota((TOK, TOK), 0) == iota((TOK, TOK), 1)).astype(BF16)
    turned = lax.dot_general(table.astype(BF16), eye, (((0,), (0,)), ((), ())), preferred_element_type=F32)
    id_rows = turned[0:2, :].astype(jnp.int32)
    expert = iota((CHIPS, TOK), 0)
    first, second = expert == id_rows[0:1, :], expert == id_rows[1:2, :]
    named = jnp.where(first | second, 1.0, 0.0)
    before = (iota((TOK, TOK), 0) < iota((TOK, TOK), 1)).astype(BF16)
    counts = jnp.dot(named.astype(BF16), before, preferred_element_type=F32)
    ranks = [jnp.sum(jnp.where(hit, counts, 0.0), axis=0, keepdims=True).astype(jnp.int32) for hit in (first, second)]
    place_of = []
    for k in range(2):
        one = id_rows[k : k + 1, :]
        dz = ((one >> 1) - z) & 7
        dx = (one & 1) ^ xh
        place_of.append(dz * 2 + dx)
    meta_rows = [place_of[0], place_of[1], ranks[0], ranks[1]]
    sub = iota((META, TOK), 0)
    meta = jnp.zeros((META, TOK), F32)
    for at, row in enumerate(meta_rows):
        meta = jnp.where(sub == at, row.astype(F32), meta)
    for at in range(4):
        meta = jnp.where(sub == 4 + at, turned[2 + at : 3 + at, :], meta)
    carried[TOK : TOK + META, :] = jnp.zeros((META, D), BF16)
    carried[TOK : TOK + META, 0:TOK] = meta.astype(BF16)
    main, rest = slot_masks(place_of, ranks, TOK)
    pick = jnp.where(main[0] | main[1], 1.0, 0.0).astype(BF16)
    packed = jnp.dot(pick, normed, preferred_element_type=F32).astype(BF16)
    for i in range(CHIPS):
        blocks[i][:, 0:D] = packed[i * MAIN : (i + 1) * MAIN, :]
    extra = jnp.zeros((CHIPS * MAIN, QUART), F32)
    for j in range(4):
        pick = jnp.where(rest[j][0] | rest[j][1], 1.0, 0.0).astype(BF16)
        extra += jnp.dot(pick, normed[:, j * QUART : (j + 1) * QUART], preferred_element_type=F32)
    extra = extra.astype(BF16)
    for i in range(CHIPS):
        blocks[i][:, D:WIDE] = extra[i * MAIN : (i + 1) * MAIN, :]


def slot_masks(place_of, ranks, tokens):
    number = {dz * 2 + dx: i for i, (dz, dx) in enumerate(ORDER)}
    main, rest = [], [[] for _ in range(4)]
    row = iota((CHIPS * MAIN, tokens), 0)
    for k in range(2):
        block = jnp.zeros_like(place_of[k])
        for relative, i in number.items():
            block = jnp.where(place_of[k] == relative, i, block)
        rank = ranks[k]
        main.append(row == jnp.where(rank < MAIN, block * MAIN + rank, -1))
        for j in range(4):
            rest[j].append(row == jnp.where(rank < MAIN, -1, block * MAIN + j * REST + rank - MAIN))
    return main, rest


def expert_kernel(count, *refs):
    own, (other, up, down) = refs[:count], refs[count : count + 3]
    mine, theirs, x, y = refs[count + 3 :]
    half, few = count * MAIN, count * REST
    for i in range(count):
        x[i * MAIN : (i + 1) * MAIN, :] = own[i][:, 0:D]
    x[half : 2 * half, :] = other[:, 0:D]
    packed = jnp.concatenate([own[i][:, D:WIDE] for i in range(count)] + [other[:, D:WIDE]], axis=0)
    row, col = iota((2 * few, 2 * half), 0), iota((2 * few, 2 * half), 1)
    start = (row // REST) * MAIN + row % REST
    for j in range(4):
        pick = (col == start + j * REST).astype(BF16)
        x[2 * half :, j * QUART : (j + 1) * QUART] = jnp.dot(pick, packed, preferred_element_type=F32).astype(BF16)
    pre = jnp.dot(x[...], up[...], preferred_element_type=F32)
    gate, value = pre[:, :H2], pre[:, H2:]
    hidden = (gate / (1.0 + jnp.exp(-gate)) * value).astype(BF16)
    y[...] = jnp.dot(hidden, down[...], preferred_element_type=F32).astype(BF16)
    mine[:, 0:D] = y[0:half, :]
    theirs[:, 0:D] = y[half : 2 * half, :]
    row, col = iota((2 * half, 2 * few), 0), iota((2 * half, 2 * few), 1)
    start = (col // REST) * MAIN + col % REST
    extra = jnp.zeros((2 * half, QUART), F32)
    for j in range(4):
        pick = (row == start + j * REST).astype(BF16)
        extra += jnp.dot(pick, y[2 * half :, j * QUART : (j + 1) * QUART], preferred_element_type=F32)
    extra = extra.astype(BF16)
    mine[:, D:WIDE] = extra[0:half, :]
    theirs[:, D:WIDE] = extra[half:, :]


def add_kernel(count, mine, got, *outs):
    for i in range(count):
        at = slice(i * MAIN, (i + 1) * MAIN)
        outs[i][...] = (mine[at, :].astype(F32) + got[at, :].astype(F32)).astype(BF16)


def combine_kernel(place, carried, *refs):
    blocks, out, main_all, rest_all = refs[:CHIPS], refs[CHIPS], refs[CHIPS + 1], refs[CHIPS + 2]
    at = pl.multiple_of(place[0], HALF)
    meta = carried[TOK : TOK + META, 0:TOK].astype(F32)
    take = (iota((TOK, HALF), 0) == iota((TOK, HALF), 1) + at).astype(BF16)
    meta = jnp.dot(meta.astype(BF16), take, preferred_element_type=F32)
    places = [meta[k : k + 1, :].astype(jnp.int32) for k in range(2)]
    ranks = [meta[2 + k : 3 + k, :].astype(jnp.int32) for k in range(2)]
    main, rest = slot_masks(places, ranks, HALF)
    for i in range(CHIPS):
        main_all[i * MAIN : (i + 1) * MAIN, :] = blocks[i][:, 0:D]
        rest_all[i * MAIN : (i + 1) * MAIN, :] = blocks[i][:, D:WIDE]

    def weighed(masks):
        both = []
        for part in range(2):
            w = [meta[4 + 2 * part + k : 5 + 2 * part + k, :] for k in range(2)]
            both.append((jnp.where(masks[0], w[0], 0.0) + jnp.where(masks[1], w[1], 0.0)).astype(BF16))
        return both

    def product(mats, rows):
        dims = (((0,), (0,)), ((), ()))
        return sum(lax.dot_general(m, rows, dims, preferred_element_type=F32) for m in mats)

    main_w = weighed(main)
    for j in range(4):
        cols = slice(j * QUART, (j + 1) * QUART)
        mixed = product(main_w, main_all[:, cols]) + product(weighed(rest[j]), rest_all[...])
        out[:, cols] = (carried[pl.ds(at, HALF), cols].astype(F32) + mixed).astype(BF16)


def moved(block, route):
    pairs = []
    for p in range(8):
        for e in range(32):
            q, z, xh, c = route(p, e // 4, (e // 2) % 2, e % 2)
            pairs.append((p * 32 + e, (q % 8) * 32 + (z % 8) * 4 + (xh % 2) * 2 + c))
    return lax.ppermute(block, ("pipe", "expert"), pairs)


def on_device(fwd_tokens, bwd_tokens, routes, route_weights, norm_gain, gate_up, down):
    spot = lax.axis_index("expert")
    core = spot % 2
    place = jnp.stack([spot // 4, (spot // 2) % 2]).astype(jnp.int32)
    shape = jax.ShapeDtypeStruct
    *blocks, carried = call(
        build_kernel,
        [shape((MAIN, WIDE), BF16)] * CHIPS + [shape((TOK + META, D), BF16)],
        [SMEM] + [VMEM] * 5,
        [VMEM] * (CHIPS + 1),
    )(place, fwd_tokens[0], bwd_tokens[0], routes[0, 0], route_weights[0, 0], norm_gain)
    got = [
        blocks[i] if ORDER[i] == (0, 0) else moved(blocks[i], lambda p, z, xh, c, o=ORDER[i]: (p, z + o[0], xh + o[1], c))
        for i in range(CHIPS)
    ]
    carried = moved(carried, lambda p, z, xh, c: (p + 1 - 2 * c, z, xh, c))
    back = [None] * CHIPS
    for group in GROUPS:
        n = len(group)
        own = [got[i] for i in group]
        other = moved(jnp.concatenate(own, axis=0), lambda p, z, xh, c: (p, z, xh, 1 - c))
        mine, theirs = call(
            functools.partial(expert_kernel, n),
            [shape((n * MAIN, WIDE), BF16)] * 2,
            [VMEM] * (n + 3),
            [VMEM] * 2,
            [pltpu.VMEM((2 * n * (MAIN + REST), D), BF16)] * 2,
        )(*own, other, gate_up[0, 0], down[0, 0])
        theirs = moved(theirs, lambda p, z, xh, c: (p, z, xh, 1 - c))
        summed = call(
            functools.partial(add_kernel, n), [shape((MAIN, WIDE), BF16)] * n, [VMEM] * 2, [VMEM] * n
        )(mine, theirs)
        for i, block in zip(group, summed):
            dz, dx = ORDER[i]
            back[i] = moved(block, lambda p, z, xh, c, dz=dz, dx=dx: (p + 1 - 2 * c, z - dz, xh + dx, c))

    def combined(start):
        return call(
            combine_kernel,
            shape((HALF, D), BF16),
            [SMEM] + [VMEM] * (CHIPS + 1),
            VMEM,
            [pltpu.VMEM((CHIPS * MAIN, D), BF16), pltpu.VMEM((CHIPS * MAIN, QUART), BF16)],
        )(start, carried, *back)

    going = combined(jnp.full((1,), HALF, jnp.int32) * (1 - core))
    staying = combined(jnp.full((1,), HALF, jnp.int32) * core)
    came = moved(going, lambda p, z, xh, c: (p - 2 + 4 * c, z, xh, c))
    fwd_next = jnp.where(core == 0, staying, came)
    bwd_next = jnp.where(core == 0, came, staying)
    return fwd_next[None], bwd_next[None]


def solution(mesh):
    in_specs = (
        P("pipe", "expert", None),
        P("pipe", "expert", None),
        P("pipe", "expert", None, None),
        P("pipe", "expert", None, None),
        P("pipe", None),
        P("pipe", "expert", None, None),
        P("pipe", "expert", None, None),
    )
    out_specs = (P("pipe", "expert", None), P("pipe", "expert", None))
    return jax.shard_map(on_device, mesh=mesh, in_specs=in_specs, out_specs=out_specs, check_vma=False)
```

```python
import functools
import jax
import jax.numpy as jnp
from jax import lax
from jax.experimental import pallas as pl
from jax.experimental.pallas import tpu as pltpu
from jax.sharding import PartitionSpec as P

D = 3584
H2 = 512
TOK = 128
HALF = 64
CHIPS = 16
MAIN = 16
REST = 4
QUART = D // 4
WIDE = D + QUART
META = 16
PART = H2 // 2
ORDER = ((1, 0), (4, 1), (7, 0), (3, 0), (0, 1), (5, 0), (2, 0), (6, 1), (4, 0), (1, 1), (7, 1), (3, 1), (5, 1), (2, 1), (6, 0), (0, 0))
VMEM = pl.BlockSpec(memory_space=pltpu.VMEM)
HBM = pl.BlockSpec(memory_space=pltpu.HBM)
SMEM = pl.BlockSpec(memory_space=pltpu.SMEM)
F32 = jnp.float32
BF16 = jnp.bfloat16


def iota(shape, axis):
    return lax.broadcasted_iota(jnp.int32, shape, axis)


def call(kernel, out_shape, in_specs, out_specs, scratch=(), limit=24):
    return pl.pallas_call(
        kernel,
        out_shape=out_shape,
        in_specs=in_specs,
        out_specs=out_specs,
        scratch_shapes=scratch,
        compiler_params=pltpu.CompilerParams(vmem_limit_bytes=limit * 2**20),
    )


def build_kernel(place, fwd, bwd, ids_hbm, weights_hbm, gain_hbm, *refs):
    send, carried, ids, weights, gain, packed, sems = refs
    loads = [
        pltpu.make_async_copy(source, target, sems.at[at])
        for at, (source, target) in enumerate(
            ((ids_hbm, ids), (weights_hbm, weights), (gain_hbm, gain), (fwd, carried.at[0:HALF, :]), (bwd, carried.at[HALF:TOK, :]))
        )
    ]
    for load in loads:
        load.start()
    for load in loads[:2]:
        load.wait()
    expert = iota((CHIPS, TOK), 0)
    hits = [expert == ids[k : k + 1, :] for k in range(2)]
    named = jnp.where(hits[0] | hits[1], 1.0, 0.0).astype(BF16)
    before = (iota((TOK, TOK), 0) < iota((TOK, TOK), 1)).astype(BF16)
    counts = jnp.dot(named, before, preferred_element_type=F32)
    ranks = [jnp.sum(jnp.where(hit, counts, 0.0), axis=0, keepdims=True) for hit in hits]
    numbers = []
    for k in range(2):
        dz, dx = ((ids[k : k + 1, :] >> 1) - place[0]) & 7, (ids[k : k + 1, :] & 1) ^ place[1]
        number = jnp.zeros_like(dz)
        for i, (one_z, one_x) in enumerate(ORDER):
            number = jnp.where((dz == one_z) & (dx == one_x), i, number)
        numbers.append(number)
    high = weights[...].astype(BF16).astype(F32)
    low = weights[...] - high
    sub = iota((META, TOK), 0)
    table = jnp.zeros((META, TOK), F32)
    entries = [numbers[0].astype(F32), numbers[1].astype(F32), *ranks, high[0:1], high[1:2], low[0:1], low[1:2]]
    for at, row in enumerate(entries):
        table = jnp.where(sub == at, row, table)
    carried[TOK : TOK + META, :] = jnp.zeros((META, D), BF16)
    carried[TOK : TOK + META, 0:TOK] = table.astype(BF16)
    main, rest = slot_masks([ids[k : k + 1, :] for k in range(2)], [r.astype(jnp.int32) for r in ranks], TOK)
    pick = jnp.where(main[0] | main[1], 1.0, 0.0).astype(BF16)
    picks = [jnp.where(rest[j][0] | rest[j][1], 1.0, 0.0).astype(BF16) for j in range(4)]
    for load in loads[2:]:
        load.wait()
    values = carried[0:TOK, :].astype(F32)
    scale = lax.rsqrt(jnp.mean(values * values, axis=-1, keepdims=True) + 1e-06)
    normed = (values * scale * gain[...]).astype(BF16)
    stores = []
    extra = jnp.zeros((CHIPS * MAIN, QUART), F32)
    for j in range(5):
        cols = slice(j * QUART, (j + 1) * QUART)
        if j < 4:
            packed[:, cols] = jnp.dot(pick, normed[:, cols], preferred_element_type=F32).astype(BF16)
            extra += jnp.dot(picks[j], normed[:, cols], preferred_element_type=F32)
        else:
            packed[:, cols] = extra.astype(BF16)
        stores.append(pltpu.make_async_copy(packed.at[:, cols], send.at[:, cols], sems.at[5 + j]))
        stores[-1].start()
    for store in stores:
        store.wait()


def slot_masks(blocks, ranks, tokens):
    main, rest = [], [[] for _ in range(4)]
    row = iota((CHIPS * MAIN, tokens), 0)
    for block, rank in zip(blocks, ranks):
        main.append(row == jnp.where(rank < MAIN, block * MAIN + rank, -1))
        for j in range(4):
            rest[j].append(row == jnp.where(rank < MAIN, -1, block * MAIN + j * REST + rank - MAIN))
    return main, rest


def build(place, *arrays):
    shape = jax.ShapeDtypeStruct
    return call(
        build_kernel,
        [pltpu.HBM((CHIPS * MAIN, WIDE), BF16), shape((TOK + META, D), BF16)],
        [SMEM] + [HBM] * 5,
        [HBM, VMEM],
        [
            pltpu.VMEM((2, TOK), jnp.int32),
            pltpu.VMEM((2, TOK), F32),
            pltpu.VMEM((1, D), F32),
            pltpu.VMEM((CHIPS * MAIN, WIDE), BF16),
            pltpu.SemaphoreType.DMA((10,)),
        ],
    )(place, *(pltpu.with_memory_space_constraint(a, pltpu.HBM) for a in arrays))


def expert_kernel(place, recv, *refs):
    ups, downs, outs = refs[0:2], refs[2:4], refs[4 : 4 + CHIPS]
    x, tails, total, wide, deep, sems = refs[4 + CHIPS :]
    rows, few = CHIPS * MAIN, CHIPS * REST

    def loads(c):
        w, at, slot = c // 2, (c % 2) * PART, c % 2
        pairs = (
            (ups[w].at[:, at : at + PART], wide.at[slot, :, 0:PART]),
            (ups[w].at[:, H2 + at : H2 + at + PART], wide.at[slot, :, PART : 2 * PART]),
            (downs[w].at[at : at + PART, :], deep.at[slot]),
        )
        return [pltpu.make_async_copy(source, target, sems.at[slot, n]) for n, (source, target) in enumerate(pairs)]

    for c in range(2):
        for load in loads(c):
            load.start()
    for i, (dz, dx) in enumerate(ORDER):
        at = pl.ds(pl.multiple_of((((place[0] - dz) & 7) * 2 + (place[1] ^ dx)) * MAIN, MAIN), MAIN)
        x[i * MAIN : (i + 1) * MAIN, :] = recv[at, 0:D]
        tails[i * MAIN : (i + 1) * MAIN, :] = recv[at, D:WIDE]
    row, col = iota((few, rows), 0), iota((few, rows), 1)
    start = (row // REST) * MAIN + row % REST
    for j in range(4):
        pick = (col == start + j * REST).astype(BF16)
        x[rows:, j * QUART : (j + 1) * QUART] = jnp.dot(pick, tails[...], preferred_element_type=F32).astype(BF16)
    for c in range(4):
        arrived = loads(c)
        arrived[0].wait()
        arrived[1].wait()
        pre = jnp.dot(x[...], wide[c % 2], preferred_element_type=F32)
        gate, value = pre[:, :PART], pre[:, PART:]
        hidden = (gate / (1.0 + jnp.exp(-gate)) * value).astype(BF16)
        arrived[2].wait()
        part = jnp.dot(hidden, deep[c % 2], preferred_element_type=F32)
        if c == 0:
            total[...] = part
        else:
            total[...] += part
        if c < 2:
            for load in loads(c + 2):
                load.start()
    row, col = iota((rows, few), 0), iota((rows, few), 1)
    start = (col // REST) * MAIN + col % REST
    picks = jnp.concatenate([(row == start + j * REST).astype(BF16) for j in range(4)], axis=1)
    rest = jnp.concatenate([total[rows:, j * QUART : (j + 1) * QUART] for j in range(4)], axis=0).astype(BF16)
    extra = jnp.dot(picks, rest, preferred_element_type=F32).astype(BF16)
    for i in range(CHIPS):
        outs[i][:, 0:D] = total[i * MAIN : (i + 1) * MAIN, :].astype(BF16)
        outs[i][:, D:WIDE] = extra[i * MAIN : (i + 1) * MAIN, :]


def expert(place, recv, ups, downs):
    shape = jax.ShapeDtypeStruct
    return call(
        expert_kernel,
        [shape((MAIN, WIDE), BF16)] * CHIPS,
        [SMEM, VMEM] + [HBM] * 4,
        [VMEM] * CHIPS,
        [
            pltpu.VMEM((CHIPS * (MAIN + REST), D), BF16),
            pltpu.VMEM((CHIPS * MAIN, QUART), BF16),
            pltpu.VMEM((CHIPS * (MAIN + REST), D), F32),
            pltpu.VMEM((2, D, 2 * PART), BF16),
            pltpu.VMEM((2, PART, D), BF16),
            pltpu.SemaphoreType.DMA((2, 3)),
        ],
        limit=32,
    )(place, recv, *(pltpu.with_memory_space_constraint(w, pltpu.HBM) for w in (*ups, *downs)))


def combine_kernel(carried, *refs):
    blocks, outs, main_all, rest_all = refs[:CHIPS], refs[CHIPS : CHIPS + 2], refs[CHIPS + 2], refs[CHIPS + 3]
    meta = carried[TOK : TOK + META, 0:TOK].astype(F32)
    numbers = [meta[k : k + 1, :].astype(jnp.int32) for k in range(2)]
    ranks = [meta[2 + k : 3 + k, :].astype(jnp.int32) for k in range(2)]
    main, rest = slot_masks(numbers, ranks, TOK)
    for i in range(CHIPS):
        main_all[i * MAIN : (i + 1) * MAIN, :] = blocks[i][:, 0:D]
        rest_all[i * MAIN : (i + 1) * MAIN, :] = blocks[i][:, D:WIDE]

    def weighed(masks):
        both = []
        for part in range(2):
            w = [meta[4 + 2 * part + k : 5 + 2 * part + k, :] for k in range(2)]
            both.append((jnp.where(masks[0], w[0], 0.0) + jnp.where(masks[1], w[1], 0.0)).astype(BF16))
        return both

    def product(mats, rows):
        dims = (((0,), (0,)), ((), ()))
        return sum(lax.dot_general(m, rows, dims, preferred_element_type=F32) for m in mats)

    main_w = weighed(main)
    for j in range(4):
        cols = slice(j * QUART, (j + 1) * QUART)
        mixed = product(main_w, main_all[:, cols]) + product(weighed(rest[j]), rest_all[...])
        updated = (carried[0:TOK, cols].astype(F32) + mixed).astype(BF16)
        outs[0][:, cols] = updated[0:HALF]
        outs[1][:, cols] = updated[HALF:TOK]


def combine(carried, blocks):
    return call(
        combine_kernel,
        [jax.ShapeDtypeStruct((HALF, D), BF16)] * 2,
        [VMEM] * (CHIPS + 1),
        [VMEM] * 2,
        [pltpu.VMEM((CHIPS * MAIN, D), BF16), pltpu.VMEM((CHIPS * MAIN, QUART), BF16)],
    )(carried, *blocks)


def moved(block, route):
    pairs = []
    for p in range(8):
        for e in range(32):
            q, z, xh, c = route(p, e // 4, (e // 2) % 2, e % 2)
            pairs.append((p * 32 + e, (q % 8) * 32 + (z % 8) * 4 + (xh % 2) * 2 + c))
    return lax.ppermute(block, ("pipe", "expert"), pairs)


def after(block, *ended):
    return lax.optimization_barrier((block, *ended))[0]


def on_device(fwd_tokens, bwd_tokens, routes, route_weights, norm_gain, gate_up, down):
    spot = lax.axis_index("expert")
    place = jnp.stack([spot // 4, (spot // 2) % 2]).astype(jnp.int32)
    send, carried = build(place, fwd_tokens[0], bwd_tokens[0], routes[0, 0].T, route_weights[0, 0].T, norm_gain)
    same_core = [[2 * i + c for i in range(CHIPS)] for c in range(2)]
    recv = lax.all_to_all(send, "expert", split_axis=0, concat_axis=0, tiled=True, axis_index_groups=same_core)
    beside = moved(carried, lambda p, z, xh, c: (p + 1 - 2 * c, z, xh, c))
    ups, downs = ([w, moved(after(w, carried), lambda p, z, xh, c: (p, z, xh, 1 - c))] for w in (gate_up[0, 0], down[0, 0]))
    recv, beside, ups, downs = lax.optimization_barrier((recv, beside, ups, downs))
    back = []
    for (dz, dx), block in zip(ORDER, expert(place, recv, ups, downs)):
        back.append(moved(block, lambda p, z, xh, c, dz=dz, dx=dx: (p + 1 - 2 * c, z - dz, xh + dx, c)))
    fwd, bwd = combine(beside, back)
    fwd_next = moved(fwd, lambda p, z, xh, c: (p + 2 * c, z, xh, c))
    bwd_next = moved(bwd, lambda p, z, xh, c: (p - 2 + 2 * c, z, xh, c))
    return fwd_next[None], bwd_next[None]


def solution(mesh):
    in_specs = (
        P("pipe", "expert", None),
        P("pipe", "expert", None),
        P("pipe", "expert", None, None),
        P("pipe", "expert", None, None),
        P("pipe", None),
        P("pipe", "expert", None, None),
        P("pipe", "expert", None, None),
    )
    out_specs = (P("pipe", "expert", None), P("pipe", "expert", None))
    return jax.shard_map(on_device, mesh=mesh, in_specs=in_specs, out_specs=out_specs, check_vma=False)
```

```python
import functools
import jax
import jax.numpy as jnp
from jax import lax
from jax.experimental import pallas as pl
from jax.experimental.pallas import tpu as pltpu
from jax.sharding import PartitionSpec as P

D = 3584
H2 = 512
TOK = 128
HALF = 64
CHIPS = 16
MAIN = 16
REST = 4
QUART = D // 4
WIDE = D + QUART
META = 16
PART = H2 // 2
ORDER = ((1, 0), (4, 1), (7, 0), (3, 0), (0, 1), (5, 0), (2, 0), (6, 1), (4, 0), (1, 1), (7, 1), (3, 1), (5, 1), (2, 1), (6, 0), (0, 0))
VMEM = pl.BlockSpec(memory_space=pltpu.VMEM)
HBM = pl.BlockSpec(memory_space=pltpu.HBM)
SMEM = pl.BlockSpec(memory_space=pltpu.SMEM)
F32 = jnp.float32
BF16 = jnp.bfloat16


def iota(shape, axis):
    return lax.broadcasted_iota(jnp.int32, shape, axis)


def call(kernel, out_shape, in_specs, out_specs, scratch=(), limit=24):
    return pl.pallas_call(
        kernel,
        out_shape=out_shape,
        in_specs=in_specs,
        out_specs=out_specs,
        scratch_shapes=scratch,
        compiler_params=pltpu.CompilerParams(vmem_limit_bytes=limit * 2**20),
    )


def build_kernel(place, fwd, bwd, ids_hbm, weights_hbm, gain_hbm, *refs):
    send, beside, carried, ids, weights, gain, packed, sems = refs
    loads = [
        pltpu.make_async_copy(source, target, sems.at[at])
        for at, (source, target) in enumerate(
            ((ids_hbm, ids), (weights_hbm, weights), (gain_hbm, gain), (fwd, carried.at[0:HALF, :]), (bwd, carried.at[HALF:TOK, :]))
        )
    ]
    for load in loads:
        load.start()
    for load in loads[:2]:
        load.wait()
    expert = iota((CHIPS, TOK), 0)
    hits = [expert == ids[k : k + 1, :] for k in range(2)]
    named = jnp.where(hits[0] | hits[1], 1.0, 0.0).astype(BF16)
    before = (iota((TOK, TOK), 0) < iota((TOK, TOK), 1)).astype(BF16)
    counts = jnp.dot(named, before, preferred_element_type=F32)
    ranks = [jnp.sum(jnp.where(hit, counts, 0.0), axis=0, keepdims=True) for hit in hits]
    numbers = []
    for k in range(2):
        dz, dx = ((ids[k : k + 1, :] >> 1) - place[0]) & 7, (ids[k : k + 1, :] & 1) ^ place[1]
        number = jnp.zeros_like(dz)
        for i, (one_z, one_x) in enumerate(ORDER):
            number = jnp.where((dz == one_z) & (dx == one_x), i, number)
        numbers.append(number)
    high = weights[...].astype(BF16).astype(F32)
    low = weights[...] - high
    sub = iota((META, TOK), 0)
    table = jnp.zeros((META, TOK), F32)
    entries = [numbers[0].astype(F32), numbers[1].astype(F32), *ranks, high[0:1], high[1:2], low[0:1], low[1:2]]
    for at, row in enumerate(entries):
        table = jnp.where(sub == at, row, table)
    carried[TOK : TOK + META, :] = jnp.zeros((META, D), BF16)
    carried[TOK : TOK + META, 0:TOK] = table.astype(BF16)
    main, rest = slot_masks([ids[k : k + 1, :] for k in range(2)], [r.astype(jnp.int32) for r in ranks], TOK)
    pick = jnp.where(main[0] | main[1], 1.0, 0.0).astype(BF16)
    picks = [jnp.where(rest[j][0] | rest[j][1], 1.0, 0.0).astype(BF16) for j in range(4)]
    for load in loads[2:]:
        load.wait()
    values = carried[0:TOK, :].astype(F32)
    scale = lax.rsqrt(jnp.mean(values * values, axis=-1, keepdims=True) + 1e-06)
    normed = (values * scale * gain[...]).astype(BF16)
    stores = [pltpu.make_async_copy(carried, beside, sems.at[10])]
    stores[0].start()
    extra = jnp.zeros((CHIPS * MAIN, QUART), F32)
    for j in range(5):
        cols = slice(j * QUART, (j + 1) * QUART)
        if j < 4:
            packed[:, cols] = jnp.dot(pick, normed[:, cols], preferred_element_type=F32).astype(BF16)
            extra += jnp.dot(picks[j], normed[:, cols], preferred_element_type=F32)
        else:
            packed[:, cols] = extra.astype(BF16)
        stores.append(pltpu.make_async_copy(packed.at[:, cols], send.at[:, cols], sems.at[5 + j]))
        stores[-1].start()
    for store in stores:
        store.wait()


def slot_masks(blocks, ranks, tokens):
    main, rest = [], [[] for _ in range(4)]
    row = iota((CHIPS * MAIN, tokens), 0)
    for block, rank in zip(blocks, ranks):
        main.append(row == jnp.where(rank < MAIN, block * MAIN + rank, -1))
        for j in range(4):
            rest[j].append(row == jnp.where(rank < MAIN, -1, block * MAIN + j * REST + rank - MAIN))
    return main, rest


def build(place, *arrays):
    return call(
        build_kernel,
        [pltpu.HBM((CHIPS * MAIN, WIDE), BF16), pltpu.HBM((TOK + META, D), BF16)],
        [SMEM] + [HBM] * 5,
        [HBM] * 2,
        [
            pltpu.VMEM((TOK + META, D), BF16),
            pltpu.VMEM((2, TOK), jnp.int32),
            pltpu.VMEM((2, TOK), F32),
            pltpu.VMEM((1, D), F32),
            pltpu.VMEM((CHIPS * MAIN, WIDE), BF16),
            pltpu.SemaphoreType.DMA((11,)),
        ],
    )(place, *(pltpu.with_memory_space_constraint(a, pltpu.HBM) for a in arrays))


def expert_kernel(place, recv, *refs):
    ups, downs, outs = refs[0:2], refs[2:4], refs[4 : 4 + CHIPS]
    x, tails, total, wide, deep, sems = refs[4 + CHIPS :]
    rows, few = CHIPS * MAIN, CHIPS * REST

    def loads(c):
        w, at, slot = c // 2, (c % 2) * PART, c % 2
        pairs = (
            (ups[w].at[:, at : at + PART], wide.at[slot, :, 0:PART]),
            (ups[w].at[:, H2 + at : H2 + at + PART], wide.at[slot, :, PART : 2 * PART]),
            (downs[w].at[at : at + PART, :], deep.at[slot]),
        )
        return [pltpu.make_async_copy(source, target, sems.at[slot, n]) for n, (source, target) in enumerate(pairs)]

    for c in range(2):
        for load in loads(c):
            load.start()
    for i, (dz, dx) in enumerate(ORDER):
        at = pl.ds(pl.multiple_of((((place[0] - dz) & 7) * 2 + (place[1] ^ dx)) * MAIN, MAIN), MAIN)
        x[i * MAIN : (i + 1) * MAIN, :] = recv[at, 0:D]
        tails[i * MAIN : (i + 1) * MAIN, :] = recv[at, D:WIDE]
    row, col = iota((few, rows), 0), iota((few, rows), 1)
    start = (row // REST) * MAIN + row % REST
    for j in range(4):
        pick = (col == start + j * REST).astype(BF16)
        x[rows:, j * QUART : (j + 1) * QUART] = jnp.dot(pick, tails[...], preferred_element_type=F32).astype(BF16)
    for c in range(4):
        arrived = loads(c)
        arrived[0].wait()
        arrived[1].wait()
        pre = jnp.dot(x[...], wide[c % 2], preferred_element_type=F32)
        gate, value = pre[:, :PART], pre[:, PART:]
        hidden = (gate / (1.0 + jnp.exp(-gate)) * value).astype(BF16)
        arrived[2].wait()
        part = jnp.dot(hidden, deep[c % 2], preferred_element_type=F32)
        if c == 0:
            total[...] = part
        else:
            total[...] += part
        if c < 2:
            for load in loads(c + 2):
                load.start()
    row, col = iota((rows, few), 0), iota((rows, few), 1)
    start = (col // REST) * MAIN + col % REST
    picks = jnp.concatenate([(row == start + j * REST).astype(BF16) for j in range(4)], axis=1)
    rest = jnp.concatenate([total[rows:, j * QUART : (j + 1) * QUART] for j in range(4)], axis=0).astype(BF16)
    extra = jnp.dot(picks, rest, preferred_element_type=F32).astype(BF16)
    for i in range(CHIPS):
        outs[i][:, 0:D] = total[i * MAIN : (i + 1) * MAIN, :].astype(BF16)
        outs[i][:, D:WIDE] = extra[i * MAIN : (i + 1) * MAIN, :]


def expert(place, recv, ups, downs):
    shape = jax.ShapeDtypeStruct
    return call(
        expert_kernel,
        [shape((MAIN, WIDE), BF16)] * CHIPS,
        [SMEM, VMEM] + [HBM] * 4,
        [VMEM] * CHIPS,
        [
            pltpu.VMEM((CHIPS * (MAIN + REST), D), BF16),
            pltpu.VMEM((CHIPS * MAIN, QUART), BF16),
            pltpu.VMEM((CHIPS * (MAIN + REST), D), F32),
            pltpu.VMEM((2, D, 2 * PART), BF16),
            pltpu.VMEM((2, PART, D), BF16),
            pltpu.SemaphoreType.DMA((2, 3)),
        ],
        limit=32,
    )(place, recv, *(pltpu.with_memory_space_constraint(w, pltpu.HBM) for w in (*ups, *downs)))


def summed(at, carried, blocks, main_all, rest_all, out):
    take = (iota((TOK, HALF), 0) == iota((TOK, HALF), 1) + at).astype(BF16)
    meta = jnp.dot(carried[TOK : TOK + META, 0:TOK], take, preferred_element_type=F32)
    numbers = [meta[k : k + 1, :].astype(jnp.int32) for k in range(2)]
    ranks = [meta[2 + k : 3 + k, :].astype(jnp.int32) for k in range(2)]
    main, rest = slot_masks(numbers, ranks, HALF)
    for i in range(CHIPS):
        main_all[i * MAIN : (i + 1) * MAIN, :] = blocks[i][:, 0:D]
        rest_all[i * MAIN : (i + 1) * MAIN, :] = blocks[i][:, D:WIDE]

    def weighed(masks):
        both = []
        for part in range(2):
            w = [meta[4 + 2 * part + k : 5 + 2 * part + k, :] for k in range(2)]
            both.append((jnp.where(masks[0], w[0], 0.0) + jnp.where(masks[1], w[1], 0.0)).astype(BF16))
        return both

    def product(mats, rows):
        dims = (((0,), (0,)), ((), ()))
        return sum(lax.dot_general(m, rows, dims, preferred_element_type=F32) for m in mats)

    main_w = weighed(main)
    for j in range(4):
        cols = slice(j * QUART, (j + 1) * QUART)
        mixed = product(main_w, main_all[:, cols]) + product(weighed(rest[j]), rest_all[...])
        out[:, cols] = (carried[pl.ds(at, HALF), cols].astype(F32) + mixed).astype(BF16)


def going_kernel(core, carried, *refs):
    at = pl.multiple_of(HALF * (1 - core[0]), HALF)
    summed(at, carried, refs[:CHIPS], refs[CHIPS + 1], refs[CHIPS + 2], refs[CHIPS])


def stored(core, rows, targets, sem):
    for c in range(2):

        @pl.when(core[0] == c)
        def _():
            copy = pltpu.make_async_copy(rows, targets[c], sem)
            copy.start()
            copy.wait()


def staying_kernel(core, carried, *refs):
    blocks, (fwd, bwd, main_all, rest_all, rows, sem) = refs[:CHIPS], refs[CHIPS:]
    summed(pl.multiple_of(HALF * core[0], HALF), carried, blocks, main_all, rest_all, rows)
    stored(core, rows, (fwd, bwd), sem)


def came_kernel(core, came, fwd_held, bwd_held, fwd, bwd, sem):
    stored(core, came, (bwd, fwd), sem)


def going(core, carried, blocks):
    scratch = [pltpu.VMEM((CHIPS * MAIN, D), BF16), pltpu.VMEM((CHIPS * MAIN, QUART), BF16)]
    out = jax.ShapeDtypeStruct((HALF, D), BF16)
    return call(going_kernel, out, [SMEM] + [VMEM] * (CHIPS + 1), VMEM, scratch)(core, carried, *blocks)


def staying(core, carried, blocks):
    scratch = [pltpu.VMEM((CHIPS * MAIN, D), BF16), pltpu.VMEM((CHIPS * MAIN, QUART), BF16)]
    scratch += [pltpu.VMEM((HALF, D), BF16), pltpu.SemaphoreType.DMA]
    out = [pltpu.HBM((HALF, D), BF16)] * 2
    return call(staying_kernel, out, [SMEM] + [VMEM] * (CHIPS + 1), [HBM] * 2, scratch)(core, carried, *blocks)


def arrive(core, came, fwd, bwd):
    return pl.pallas_call(
        came_kernel,
        out_shape=[pltpu.HBM((HALF, D), BF16)] * 2,
        in_specs=[SMEM, VMEM, HBM, HBM],
        out_specs=[HBM] * 2,
        scratch_shapes=[pltpu.SemaphoreType.DMA],
        input_output_aliases={2: 0, 3: 1},
        compiler_params=pltpu.CompilerParams(vmem_limit_bytes=4 * 2**20),
    )(core, came, fwd, bwd)


def moved(block, route):
    pairs = []
    for p in range(8):
        for e in range(32):
            q, z, xh, c = route(p, e // 4, (e // 2) % 2, e % 2)
            pairs.append((p * 32 + e, (q % 8) * 32 + (z % 8) * 4 + (xh % 2) * 2 + c))
    return lax.ppermute(block, ("pipe", "expert"), pairs)


def after(block, *ended):
    return lax.optimization_barrier((block, *ended))[0]


def on_device(fwd_tokens, bwd_tokens, routes, route_weights, norm_gain, gate_up, down):
    spot = lax.axis_index("expert")
    place = jnp.stack([spot // 4, (spot // 2) % 2]).astype(jnp.int32)
    send, carried = build(place, fwd_tokens[0], bwd_tokens[0], routes[0, 0].T, route_weights[0, 0].T, norm_gain)
    same_core = [[2 * i + c for i in range(CHIPS)] for c in range(2)]
    recv = lax.all_to_all(send, "expert", split_axis=0, concat_axis=0, tiled=True, axis_index_groups=same_core)
    beside = moved(carried, lambda p, z, xh, c: (p + 1 - 2 * c, z, xh, c))
    ups, downs = ([w, moved(after(w, carried), lambda p, z, xh, c: (p, z, xh, 1 - c))] for w in (gate_up[0, 0], down[0, 0]))
    recv, beside, ups, downs = lax.optimization_barrier((recv, beside, ups, downs))
    back = []
    for (dz, dx), block in zip(ORDER, expert(place, recv, ups, downs)):
        back.append(moved(block, lambda p, z, xh, c, dz=dz, dx=dx: (p + 1 - 2 * c, z - dz, xh + dx, c)))
    core = (spot % 2).astype(jnp.int32).reshape(1)
    came = moved(going(core, beside, back), lambda p, z, xh, c: (p - 2 + 4 * c, z, xh, c))
    fwd_next, bwd_next = arrive(core, came, *staying(core, beside, back))
    return fwd_next[None], bwd_next[None]


def solution(mesh):
    in_specs = (
        P("pipe", "expert", None),
        P("pipe", "expert", None),
        P("pipe", "expert", None, None),
        P("pipe", "expert", None, None),
        P("pipe", None),
        P("pipe", "expert", None, None),
        P("pipe", "expert", None, None),
    )
    out_specs = (P("pipe", "expert", None), P("pipe", "expert", None))
    return jax.shard_map(on_device, mesh=mesh, in_specs=in_specs, out_specs=out_specs, check_vma=False)
```

```python
import functools
import jax
import jax.numpy as jnp
from jax import lax
from jax.experimental import pallas as pl
from jax.experimental.pallas import tpu as pltpu
from jax.sharding import PartitionSpec as P

D = 3584
H2 = 512
TOK = 128
HALF = 64
CHIPS = 16
MAIN = 16
REST = 4
QUART = D // 4
WIDE = D + QUART
META = 16
PART = H2 // 2
ORDER = ((1, 0), (4, 1), (7, 0), (3, 0), (0, 1), (5, 0), (2, 0), (6, 1), (4, 0), (1, 1), (7, 1), (3, 1), (5, 1), (2, 1), (6, 0), (0, 0))
VMEM = pl.BlockSpec(memory_space=pltpu.VMEM)
HBM = pl.BlockSpec(memory_space=pltpu.HBM)
SMEM = pl.BlockSpec(memory_space=pltpu.SMEM)
F32 = jnp.float32
BF16 = jnp.bfloat16


def iota(shape, axis):
    return lax.broadcasted_iota(jnp.int32, shape, axis)


def call(kernel, out_shape, in_specs, out_specs, scratch=(), limit=24):
    return pl.pallas_call(
        kernel,
        out_shape=out_shape,
        in_specs=in_specs,
        out_specs=out_specs,
        scratch_shapes=scratch,
        compiler_params=pltpu.CompilerParams(vmem_limit_bytes=limit * 2**20),
    )


def build_kernel(place, fwd, bwd, ids_hbm, weights_hbm, gain_hbm, *refs):
    send, beside, carried, ids, weights, gain, packed, sems = refs
    loads = [
        pltpu.make_async_copy(source, target, sems.at[at])
        for at, (source, target) in enumerate(
            ((ids_hbm, ids), (weights_hbm, weights), (gain_hbm, gain), (fwd, carried.at[0:HALF, :]), (bwd, carried.at[HALF:TOK, :]))
        )
    ]
    for load in loads:
        load.start()
    for load in loads[:2]:
        load.wait()
    expert = iota((CHIPS, TOK), 0)
    hits = [expert == ids[k : k + 1, :] for k in range(2)]
    named = jnp.where(hits[0] | hits[1], 1.0, 0.0).astype(BF16)
    before = (iota((TOK, TOK), 0) < iota((TOK, TOK), 1)).astype(BF16)
    counts = jnp.dot(named, before, preferred_element_type=F32)
    ranks = [jnp.sum(jnp.where(hit, counts, 0.0), axis=0, keepdims=True) for hit in hits]
    numbers = []
    for k in range(2):
        dz, dx = ((ids[k : k + 1, :] >> 1) - place[0]) & 7, (ids[k : k + 1, :] & 1) ^ place[1]
        number = jnp.zeros_like(dz)
        for i, (one_z, one_x) in enumerate(ORDER):
            number = jnp.where((dz == one_z) & (dx == one_x), i, number)
        numbers.append(number)
    high = weights[...].astype(BF16).astype(F32)
    low = weights[...] - high
    sub = iota((META, TOK), 0)
    table = jnp.zeros((META, TOK), F32)
    entries = [numbers[0].astype(F32), numbers[1].astype(F32), *ranks, high[0:1], high[1:2], low[0:1], low[1:2]]
    for at, row in enumerate(entries):
        table = jnp.where(sub == at, row, table)
    carried[TOK : TOK + META, :] = jnp.zeros((META, D), BF16)
    carried[TOK : TOK + META, 0:TOK] = table.astype(BF16)
    main, rest = slot_masks([ids[k : k + 1, :] for k in range(2)], [r.astype(jnp.int32) for r in ranks], TOK)
    pick = jnp.where(main[0] | main[1], 1.0, 0.0).astype(BF16)
    picks = [jnp.where(rest[j][0] | rest[j][1], 1.0, 0.0).astype(BF16) for j in range(4)]
    for load in loads[2:]:
        load.wait()
    values = carried[0:TOK, :].astype(F32)
    scale = lax.rsqrt(jnp.mean(values * values, axis=-1, keepdims=True) + 1e-06)
    normed = (values * scale * gain[...]).astype(BF16)
    stores = [pltpu.make_async_copy(carried, beside, sems.at[10])]
    stores[0].start()
    extra = jnp.zeros((CHIPS * MAIN, QUART), F32)
    for j in range(5):
        cols = slice(j * QUART, (j + 1) * QUART)
        if j < 4:
            packed[:, cols] = jnp.dot(pick, normed[:, cols], preferred_element_type=F32).astype(BF16)
            extra += jnp.dot(picks[j], normed[:, cols], preferred_element_type=F32)
        else:
            packed[:, cols] = extra.astype(BF16)
        stores.append(pltpu.make_async_copy(packed.at[:, cols], send.at[:, cols], sems.at[5 + j]))
        stores[-1].start()
    for store in stores:
        store.wait()


def slot_masks(blocks, ranks, tokens):
    main, rest = [], [[] for _ in range(4)]
    row = iota((CHIPS * MAIN, tokens), 0)
    for block, rank in zip(blocks, ranks):
        main.append(row == jnp.where(rank < MAIN, block * MAIN + rank, -1))
        for j in range(4):
            rest[j].append(row == jnp.where(rank < MAIN, -1, block * MAIN + j * REST + rank - MAIN))
    return main, rest


def build(place, *arrays):
    return call(
        build_kernel,
        [pltpu.HBM((CHIPS * MAIN, WIDE), BF16), pltpu.HBM((TOK + META, D), BF16)],
        [SMEM] + [HBM] * 5,
        [HBM] * 2,
        [
            pltpu.VMEM((TOK + META, D), BF16),
            pltpu.VMEM((2, TOK), jnp.int32),
            pltpu.VMEM((2, TOK), F32),
            pltpu.VMEM((1, D), F32),
            pltpu.VMEM((CHIPS * MAIN, WIDE), BF16),
            pltpu.SemaphoreType.DMA((11,)),
        ],
    )(place, *(pltpu.with_memory_space_constraint(a, pltpu.HBM) for a in arrays))


def expert_kernel(place, recv, *refs):
    ups, downs, outs = refs[0:2], refs[2:4], refs[4 : 4 + CHIPS]
    x, tails, total, wide, deep, sems = refs[4 + CHIPS :]
    rows, few = CHIPS * MAIN, CHIPS * REST

    def loads(c):
        w, at, slot = c // 2, (c % 2) * PART, c % 2
        pairs = (
            (ups[w].at[:, at : at + PART], wide.at[slot, :, 0:PART]),
            (ups[w].at[:, H2 + at : H2 + at + PART], wide.at[slot, :, PART : 2 * PART]),
            (downs[w].at[at : at + PART, :], deep.at[slot]),
        )
        return [pltpu.make_async_copy(source, target, sems.at[slot, n]) for n, (source, target) in enumerate(pairs)]

    for c in range(2):
        for load in loads(c):
            load.start()
    for i, (dz, dx) in enumerate(ORDER):
        at = pl.ds(pl.multiple_of((((place[0] - dz) & 7) * 2 + (place[1] ^ dx)) * MAIN, MAIN), MAIN)
        x[i * MAIN : (i + 1) * MAIN, :] = recv[at, 0:D]
        tails[i * MAIN : (i + 1) * MAIN, :] = recv[at, D:WIDE]
    row, col = iota((few, rows), 0), iota((few, rows), 1)
    start = (row // REST) * MAIN + row % REST
    for j in range(4):
        pick = (col == start + j * REST).astype(BF16)
        x[rows:, j * QUART : (j + 1) * QUART] = jnp.dot(pick, tails[...], preferred_element_type=F32).astype(BF16)
    for c in range(4):
        arrived = loads(c)
        arrived[0].wait()
        arrived[1].wait()
        pre = jnp.dot(x[...], wide[c % 2], preferred_element_type=F32)
        gate, value = pre[:, :PART], pre[:, PART:]
        hidden = (gate / (1.0 + jnp.exp(-gate)) * value).astype(BF16)
        arrived[2].wait()
        part = jnp.dot(hidden, deep[c % 2], preferred_element_type=F32)
        if c == 0:
            total[...] = part
        else:
            total[...] += part
        if c < 2:
            for load in loads(c + 2):
                load.start()
    row, col = iota((rows, few), 0), iota((rows, few), 1)
    start = (col // REST) * MAIN + col % REST
    picks = jnp.concatenate([(row == start + j * REST).astype(BF16) for j in range(4)], axis=1)
    rest = jnp.concatenate([total[rows:, j * QUART : (j + 1) * QUART] for j in range(4)], axis=0).astype(BF16)
    extra = jnp.dot(picks, rest, preferred_element_type=F32).astype(BF16)
    for i in range(CHIPS):
        outs[i][:, 0:D] = total[i * MAIN : (i + 1) * MAIN, :].astype(BF16)
        outs[i][:, D:WIDE] = extra[i * MAIN : (i + 1) * MAIN, :]


def expert(place, recv, ups, downs):
    shape = jax.ShapeDtypeStruct
    return call(
        expert_kernel,
        [shape((MAIN, WIDE), BF16)] * CHIPS,
        [SMEM, VMEM] + [HBM] * 4,
        [VMEM] * CHIPS,
        [
            pltpu.VMEM((CHIPS * (MAIN + REST), D), BF16),
            pltpu.VMEM((CHIPS * MAIN, QUART), BF16),
            pltpu.VMEM((CHIPS * (MAIN + REST), D), F32),
            pltpu.VMEM((2, D, 2 * PART), BF16),
            pltpu.VMEM((2, PART, D), BF16),
            pltpu.SemaphoreType.DMA((2, 3)),
        ],
        limit=32,
    )(place, recv, *(pltpu.with_memory_space_constraint(w, pltpu.HBM) for w in (*ups, *downs)))


def summed(at, carried, blocks, main_all, rest_all, out, quarters):
    take = (iota((TOK, HALF), 0) == iota((TOK, HALF), 1) + at).astype(BF16)
    meta = jnp.dot(carried[TOK : TOK + META, 0:TOK], take, preferred_element_type=F32)
    numbers = [meta[k : k + 1, :].astype(jnp.int32) for k in range(2)]
    ranks = [meta[2 + k : 3 + k, :].astype(jnp.int32) for k in range(2)]
    main, rest = slot_masks(numbers, ranks, HALF)
    for i in range(CHIPS):
        main_all[i * MAIN : (i + 1) * MAIN, :] = blocks[i][:, quarters[0] * QUART : (quarters[-1] + 1) * QUART]
        rest_all[i * MAIN : (i + 1) * MAIN, :] = blocks[i][:, D:WIDE]

    def weighed(masks):
        both = []
        for part in range(2):
            w = [meta[4 + 2 * part + k : 5 + 2 * part + k, :] for k in range(2)]
            both.append((jnp.where(masks[0], w[0], 0.0) + jnp.where(masks[1], w[1], 0.0)).astype(BF16))
        return both

    def product(mats, rows):
        dims = (((0,), (0,)), ((), ()))
        return sum(lax.dot_general(m, rows, dims, preferred_element_type=F32) for m in mats)

    main_w = weighed(main)
    for n, j in enumerate(quarters):
        near, cols = slice(n * QUART, (n + 1) * QUART), slice(j * QUART, (j + 1) * QUART)
        mixed = product(main_w, main_all[:, near]) + product(weighed(rest[j]), rest_all[...])
        out[:, near] = (carried[pl.ds(at, HALF), cols].astype(F32) + mixed).astype(BF16)


def going_kernel(quarters, core, carried, *refs):
    at = pl.multiple_of(HALF * (1 - core[0]), HALF)
    summed(at, carried, refs[:CHIPS], refs[CHIPS + 1], refs[CHIPS + 2], refs[CHIPS], quarters)


def stored(core, pairs, sems):
    for c in range(2):

        @pl.when(core[0] == c)
        def _():
            copies = [pltpu.make_async_copy(rows, targets[c], sems.at[n]) for n, (rows, targets) in enumerate(pairs)]
            for copy in copies:
                copy.start()
            for copy in copies:
                copy.wait()


def staying_kernel(core, carried, *refs):
    blocks, (fwd, bwd, main_all, rest_all, rows, sem) = refs[:CHIPS], refs[CHIPS:]
    summed(pl.multiple_of(HALF * core[0], HALF), carried, blocks, main_all, rest_all, rows, range(4))
    stored(core, [(rows, (fwd, bwd))], sem)


def came_kernel(core, low, high, fwd_held, bwd_held, fwd, bwd, sems):
    cut = D // 2
    pairs = [(low, (bwd.at[:, 0:cut], fwd.at[:, 0:cut])), (high, (bwd.at[:, cut:D], fwd.at[:, cut:D]))]
    stored(core, pairs, sems)


def going(core, carried, blocks, quarters):
    width = len(quarters) * QUART
    scratch = [pltpu.VMEM((CHIPS * MAIN, width), BF16), pltpu.VMEM((CHIPS * MAIN, QUART), BF16)]
    kernel = functools.partial(going_kernel, quarters)
    return call(kernel, jax.ShapeDtypeStruct((HALF, width), BF16), [SMEM] + [VMEM] * (CHIPS + 1), VMEM, scratch)(core, carried, *blocks)


def staying(core, carried, blocks):
    scratch = [pltpu.VMEM((CHIPS * MAIN, D), BF16), pltpu.VMEM((CHIPS * MAIN, QUART), BF16)]
    scratch += [pltpu.VMEM((HALF, D), BF16), pltpu.SemaphoreType.DMA((1,))]
    out = [pltpu.HBM((HALF, D), BF16)] * 2
    return call(staying_kernel, out, [SMEM] + [VMEM] * (CHIPS + 1), [HBM] * 2, scratch)(core, carried, *blocks)


def arrive(core, low, high, fwd, bwd):
    return pl.pallas_call(
        came_kernel,
        out_shape=[pltpu.HBM((HALF, D), BF16)] * 2,
        in_specs=[SMEM, VMEM, VMEM, HBM, HBM],
        out_specs=[HBM] * 2,
        scratch_shapes=[pltpu.SemaphoreType.DMA((2,))],
        input_output_aliases={3: 0, 4: 1},
        compiler_params=pltpu.CompilerParams(vmem_limit_bytes=4 * 2**20),
    )(core, low, high, fwd, bwd)


def moved(block, route):
    pairs = []
    for p in range(8):
        for e in range(32):
            q, z, xh, c = route(p, e // 4, (e // 2) % 2, e % 2)
            pairs.append((p * 32 + e, (q % 8) * 32 + (z % 8) * 4 + (xh % 2) * 2 + c))
    return lax.ppermute(block, ("pipe", "expert"), pairs)


def after(block, *ended):
    return lax.optimization_barrier((block, *ended))[0]


def on_device(fwd_tokens, bwd_tokens, routes, route_weights, norm_gain, gate_up, down):
    spot = lax.axis_index("expert")
    place = jnp.stack([spot // 4, (spot // 2) % 2]).astype(jnp.int32)
    send, carried = build(place, fwd_tokens[0], bwd_tokens[0], routes[0, 0].T, route_weights[0, 0].T, norm_gain)
    same_core = [[2 * i + c for i in range(CHIPS)] for c in range(2)]
    recv = lax.all_to_all(send, "expert", split_axis=0, concat_axis=0, tiled=True, axis_index_groups=same_core)
    beside = moved(carried, lambda p, z, xh, c: (p + 1 - 2 * c, z, xh, c))
    ups, downs = ([w, moved(after(w, carried), lambda p, z, xh, c: (p, z, xh, 1 - c))] for w in (gate_up[0, 0], down[0, 0]))
    recv, beside, ups, downs = lax.optimization_barrier((recv, beside, ups, downs))
    back = []
    for (dz, dx), block in zip(ORDER, expert(place, recv, ups, downs)):
        back.append(moved(block, lambda p, z, xh, c, dz=dz, dx=dx: (p + 1 - 2 * c, z - dz, xh + dx, c)))
    core = (spot % 2).astype(jnp.int32).reshape(1)
    came = [
        moved(going(core, beside, back, quarters), lambda p, z, xh, c: (p - 2 + 4 * c, z, xh, c)) for quarters in (range(0, 2), range(2, 4))
    ]
    fwd_next, bwd_next = arrive(core, *came, *staying(core, beside, back))
    return fwd_next[None], bwd_next[None]


def solution(mesh):
    in_specs = (
        P("pipe", "expert", None),
        P("pipe", "expert", None),
        P("pipe", "expert", None, None),
        P("pipe", "expert", None, None),
        P("pipe", None),
        P("pipe", "expert", None, None),
        P("pipe", "expert", None, None),
    )
    out_specs = (P("pipe", "expert", None), P("pipe", "expert", None))
    return jax.shard_map(on_device, mesh=mesh, in_specs=in_specs, out_specs=out_specs, check_vma=False)
```
